32 devices in a mesh: xy: 8 (over z, y), gz: 4 (over x, core).
Axes of the slice: x: 2, y: 2, z: 4, core: 2. Of those that a mesh axis runs over, the one named last changes fastest.
Arguments:
- base_field: bfloat16 [132, 32, 32, 256], P(None, 'gz', 'xy'), may hold values from 0 to 2
- increments: bfloat16 [132, 262144], P(None, ('xy', 'gz')), may hold values from -6 to 6
- dest_tile: int32 [262144, 1], P(('xy', 'gz')), may hold values from 0 to 7; in each aligned block of 8192 rows (0 to 8191, 8192 to 16383, ...) at most 2048 rows name the same one
- dest_cell: int32 [262144], P(('xy', 'gz')), may hold values from 0 to 8191
- courant_x: bfloat16 [32, 32, 256], P('gz', 'xy'), may hold values from -0.23925781 to 0.23925781
- courant_y: bfloat16 [32, 32, 256], P('gz', 'xy'), may hold values from -0.23925781 to 0.23925781
- fall_courant: float32 [132, 32], replicated, may hold values from 0.001 to 280
Outputs:
- settled: bfloat16 [132, 32, 32, 256], P(None, 'gz', 'xy')
The draws below stay inside these ranges and needn't reach their ends.
Inputs may be any that keep to these rules, and one draw needn't show every extreme that they name: `dest_tile`: among the rows of one device, at most 2048 name the same tile; in every draw some device has exactly 2048 rows naming one tile.
All inputs are finite; a program needn't handle non-finite values.
Results may differ from the reference program's by a relative error of at most 0.0043.
Values may be sent and summed in bfloat16 or wider, within the bound.
A program may use at most 128 MiB of HBM per device.

```python
import math
import jax
import jax.numpy as jnp
import numpy as np
from jax import lax

SPECTRUM_BINS = 132
TX = 4
TY = 256
LZ = 8
RD = 8192
CAP = 2048
X = 32
VERTICAL_LEVELS = 32
ROWS = 262144
N_XY = 8
N_GZ = 4


def draw_fall_courant(key, part):
    velocity_random_key, level_random_key, gust_random_key, location_random_key = jax.random.split(jax.random.fold_in(key, 17), 4)
    lower_log = math.log(0.5)
    terminal_velocity = jnp.exp(jax.random.uniform(velocity_random_key, (SPECTRUM_BINS, 1), jnp.float32, lower_log, math.log(200.0)))
    speed_multiplier = jnp.exp(jax.random.uniform(level_random_key, (SPECTRUM_BINS, VERTICAL_LEVELS), jnp.float32, math.log(0.7), math.log(1.4)))
    gust_level_rows = jax.random.randint(location_random_key, (3,), 0, VERTICAL_LEVELS)
    gust_event_mask = jnp.any(lax.broadcasted_iota(jnp.int32, (VERTICAL_LEVELS, 3), 0) == gust_level_rows[None, :], axis=1)
    gust_event = jnp.exp(jax.random.uniform(gust_random_key, (SPECTRUM_BINS, VERTICAL_LEVELS), jnp.float32, math.log(0.004), math.log(0.01)))
    return terminal_velocity * speed_multiplier * jnp.where(gust_event_mask[None, :], gust_event, 1.0)


def with_ends(values, own_key, smallest, largest):
    dims = values.shape
    spot = [jax.random.randint(jax.random.fold_in(own_key, axis), (), 0, dims[axis]) for axis in range(len(dims))]
    values = values.at[tuple(spot)].set(smallest)
    longest = dims.index(max(dims))
    spot[longest] = (spot[longest] + 1) % dims[longest]
    return values.at[tuple(spot)].set(largest)


def levels(own_key, shape, cuts, least, high):
    factor_of = 1.0
    for position, parts in cuts:
        draws = jax.random.uniform(jax.random.fold_in(jax.random.fold_in(own_key, 6), position), (parts,), jnp.float32, least / len(cuts), high / len(cuts))
        factor_of = factor_of * jnp.repeat(jnp.exp(draws), shape[position] // parts).reshape((-1,) + (1,) * (len(shape) - 1 - position))
    return factor_of


def shared_out(own_key, own, number, rows, amount, top, most, lean):
    order = jax.random.permutation(own_key, amount)
    heavy_load, ordinary = shares(amount, rows * top, most, lean, True), shares(amount, rows * top, most, lean, False)
    places = jnp.arange(amount)

    def named(lengths, rotation):
        used = int((lengths > 0).sum())
        fixed = max(1, used // 4)
        moved = fixed + (places - fixed + rotation * (used - fixed)) % max(1, amount - fixed)
        return jnp.zeros((amount,), jnp.int32).at[order[jnp.where(places < fixed, places, moved)]].set(jnp.asarray(lengths, jnp.int32))

    lengths = jnp.where(number % 4 == 0, named(heavy_load, number // 4), named(ordinary, number - number // 4 - 1))
    mixed = jax.random.permutation(jax.random.fold_in(own, 3), amount)
    donor, taker = mixed[0:amount // 2 * 2:2], mixed[1:amount // 2 * 2:2]
    room = jnp.minimum(lengths[donor] - 1, most - lengths[taker]) // 2
    room = jnp.where((donor == order[0]) | (taker == order[0]) | (lengths[taker] == 0), 0, jnp.maximum(room, 0))
    moved = jax.random.randint(jax.random.fold_in(own, 4), (amount // 2,), 0, 1 << 20) % (room + 1)
    lengths = lengths.at[donor].add(-moved).at[taker].add(moved)
    items = jnp.searchsorted(jnp.cumsum(lengths), jnp.arange(rows * top), side="right").astype(jnp.int32)
    grid = items.reshape(top, rows).T
    grid = grid[jax.random.permutation(jax.random.fold_in(own, 1), rows)]
    rotation = jax.random.randint(jax.random.fold_in(own, 2), (rows, 1), 0, top)
    return jnp.take_along_axis(grid, (jnp.arange(top)[None, :] + rotation) % top, axis=1)


def shares(amount, total, reach, skew, full):
    portions = [(1 << 20) // math.isqrt(standing ** skew) + 1 for standing in range(1, amount + 1)]
    largest = reach if full else min(reach, max(-(-total // amount), total * portions[0] // sum(portions)))
    least = 1 if total - largest >= amount - 1 else 0
    given, rest = [largest] + [least] * (amount - 1), total - largest - least * (amount - 1)
    while rest > 0:
        movable = [i for i in range(1, amount) if given[i] < largest] or [i for i in range(1, amount) if given[i] < reach]
        whole, remaining = sum([portions[i] for i in movable]), rest
        for i in movable:
            extra = min(reach - given[i], max(1, remaining * portions[i] // whole), rest)
            given[i] = given[i] + extra
            rest = rest - extra
    return np.array(given)


def normal_values(own_key, dims, deviation, most, pieces=(), kind=jnp.bfloat16):
    drawn = jax.random.normal(own_key, dims, jnp.float32) * deviation
    if len(pieces) > 0:
        drawn = levels(own_key, dims, pieces, -0.22, 0.18) * drawn
    return jnp.clip(drawn, min=-most, max=most).astype(kind)


def setup_inputs(seed: int = 0) -> dict:
    splits = jax.random.split(jax.random.key(seed), 8)
    base_field = jnp.clip(2.0 * jax.random.uniform(splits[0], (SPECTRUM_BINS, VERTICAL_LEVELS, X, TY), jnp.float32) ** levels(splits[0], (SPECTRUM_BINS, VERTICAL_LEVELS, X, TY), ((1, 4), (2, 8)), -0.2, 0.2), 0.0, 2.0).astype(jnp.bfloat16)
    increments = normal_values(splits[1], (SPECTRUM_BINS, ROWS), 1.0, 6.0, ((1, 32),))
    dest_tile_keys = jax.random.split(jax.random.fold_in(splits[2], 1), ROWS // RD)
    dest_tile_turns = jax.random.permutation(jax.random.fold_in(splits[2], 3), ROWS // RD)
    dest_tile = jax.vmap(lambda own, number: shared_out(jax.random.fold_in(splits[2], 2), own, number, RD, N_XY, 1, CAP, 2))(dest_tile_keys, dest_tile_turns).reshape((ROWS, 1))
    dest_cell = with_ends(jax.random.randint(splits[3], (ROWS,), 0, LZ * TX * TY), jax.random.fold_in(splits[3], 1), 0, (LZ * TX * TY) - 1).astype(jnp.int32)
    courant_x = jnp.clip(jax.random.uniform(splits[4], (VERTICAL_LEVELS, X, TY), jnp.float32, -0.23925781, 0.23925781) * levels(splits[4], (VERTICAL_LEVELS, X, TY), ((0, 4), (1, 8)), -0.4, 0.0), -0.23925781, 0.23925781).astype(jnp.bfloat16)
    courant_y = jnp.clip(jax.random.uniform(splits[5], (VERTICAL_LEVELS, X, TY), jnp.float32, -0.23925781, 0.23925781) * levels(splits[5], (VERTICAL_LEVELS, X, TY), ((0, 4), (1, 8)), -0.4, 0.0), -0.23925781, 0.23925781).astype(jnp.bfloat16)
    fall_courant = draw_fall_courant(jax.random.fold_in(splits[7], 71), 0)
    return dict(base_field=base_field, increments=increments, dest_tile=dest_tile, dest_cell=dest_cell, courant_x=courant_x, courant_y=courant_y, fall_courant=fall_courant)


def reference(base_field, increments, dest_tile, dest_cell, courant_x, courant_y, fall_courant):
    row_total = increments.shape[1]
    slab_index = (jnp.arange(row_total, dtype=jnp.int32) // RD) % N_GZ
    cell_index = dest_cell.astype(jnp.int32)
    level_index = slab_index * LZ + cell_index // (TX * TY)
    x_index = dest_tile[:, 0].astype(jnp.int32) * TX + (cell_index // TY) % TX
    y_index = cell_index % TY
    flat_index = (level_index * X + x_index) * TY + y_index
    face_x = courant_x.astype(jnp.float32)
    face_y = courant_y.astype(jnp.float32)

    def per_component(operands):
        base_part, increment, fall_rates = operands
        summed = jnp.zeros((VERTICAL_LEVELS * X * TY,), jnp.float32).at[flat_index].add(increment.astype(jnp.float32))
        updated = (base_part.astype(jnp.float32) + summed.reshape(VERTICAL_LEVELS, X, TY)).astype(jnp.bfloat16)
        updated = lax.optimization_barrier(updated)
        current = updated.astype(jnp.float32)
        from_left = jnp.pad(current, ((0, 0), (1, 0), (0, 0)))[:, :-1, :]
        flux_west = jnp.maximum(face_x, 0.0) * from_left + jnp.minimum(face_x, 0.0) * current
        flux_west = flux_west.at[:, 0, :].set(jnp.zeros((VERTICAL_LEVELS, TY), jnp.float32))
        flux_east = jnp.pad(flux_west[:, 1:, :], ((0, 0), (0, 1), (0, 0)))
        from_below = jnp.pad(current, ((0, 0), (0, 0), (1, 0)))[:, :, :-1]
        flux_south = jnp.maximum(face_y, 0.0) * from_below + jnp.minimum(face_y, 0.0) * current
        flux_south = flux_south.at[:, :, 0].set(jnp.zeros((VERTICAL_LEVELS, X), jnp.float32))
        flux_north = jnp.pad(flux_south[:, :, 1:], ((0, 0), (0, 0), (0, 1)))
        advected = (current - (flux_east - flux_west) - (flux_north - flux_south)).astype(jnp.bfloat16)
        advected = lax.optimization_barrier(advected)
        advected = advected.astype(jnp.float32)

        def descend(inflow, operands_level):
            layer, courant = operands_level
            value = (layer + inflow) / (1.0 + courant)
            return courant * value, value

        start = jnp.zeros((X, TY), jnp.float32)
        unused, outputs = lax.scan(descend, start, (advected[::-1], fall_rates[::-1]))
        return outputs[::-1].astype(jnp.bfloat16)

    return lax.map(per_component, (base_field, increments, fall_courant))
```

```python
import functools

import jax
import jax.numpy as jnp
from jax import lax
from jax.experimental import pallas as pl
from jax.experimental.pallas import tpu as pltpu
from jax.sharding import PartitionSpec as P

MESH = pl.DeviceIdType.MESH
NT = (((1,), (1,)), ((), ()))


def up(value, multiple):
    return -(-value // multiple) * multiple


def running_counts(member):
    tiles, count = member.shape
    run = 128
    grouped = member.astype(jnp.bfloat16).reshape(tiles * (count // run), run)
    inside = jnp.dot(
        grouped, jnp.triu(jnp.ones((run, run), jnp.bfloat16)), preferred_element_type=jnp.float32
    ).reshape(tiles, count // run, run)
    before = jnp.dot(
        inside[:, :, run - 1].astype(jnp.bfloat16),
        jnp.triu(jnp.ones((count // run, count // run), jnp.bfloat16), 1),
        preferred_element_type=jnp.float32,
    )
    return (inside + before[:, :, None]).reshape(tiles, count).astype(jnp.int32)


def pack_kernel(block, starts_ref, rows_ref, slot_ref, out_ref):
    peers, height, capacity = out_ref.shape
    width = min(256, capacity)
    blocks = rows_ref.shape[1] // block
    window = lax.broadcasted_iota(jnp.int32, (width, block), 0)

    def clear(tile, carry):
        out_ref[tile] = jnp.zeros((height, capacity), out_ref.dtype)
        return carry

    lax.fori_loop(0, peers, clear, 0)

    def step(counter, carry):
        part, tile = counter // peers, counter % peers
        columns = pl.ds(pl.multiple_of(part * block, block), block)
        first = starts_ref[tile, part]
        last = starts_ref[tile, part + 1]

        def place(chunk, inner):
            base = tile * capacity + chunk * width
            match = jnp.where(window == slot_ref[:, columns] - base, 1.0, 0.0).astype(jnp.bfloat16)
            moved = lax.dot_general(
                rows_ref[:, columns], match, NT, preferred_element_type=jnp.float32
            )
            spot = pl.ds(pl.multiple_of(chunk * width, width), width)
            out_ref[tile, :, spot] += moved.astype(out_ref.dtype)
            return inner

        stop = jnp.where(last > first, (last - 1) // width + 1, first // width)
        lax.fori_loop(first // width, stop, place, 0)
        return carry

    lax.fori_loop(0, blocks * peers, step, 0)


def main_kernel(
    comps, packed, base, cx, cy, scale, gain, out, arrived, total, updated, advected, left, right,
    next_cx, flow, inflow, send_sem, recv_sem, halo_send, halo_recv, flow_send, flow_recv,
):
    peers, height, capacity = packed.shape
    xcells, levels, _, width = updated.shape
    slabs = lax.axis_size("gz")
    me, slab = lax.axis_index("xy"), lax.axis_index("gz")
    has_prev, has_next = me > 0, me < peers - 1
    has_below, has_above = slab > 0, slab < slabs - 1
    groups = xcells * levels

    barrier = pltpu.get_barrier_semaphore()

    def greet(step, carry):
        pl.semaphore_signal(
            barrier, inc=1, device_id=((me + step) % peers, slab), device_id_type=MESH
        )
        return carry

    lax.fori_loop(1, peers, greet, 0)

    @pl.when(has_below)
    def _():
        pl.semaphore_signal(barrier, inc=1, device_id=(me, slab - 1), device_id_type=MESH)

    @pl.when(has_above)
    def _():
        pl.semaphore_signal(barrier, inc=1, device_id=(me, slab + 1), device_id_type=MESH)

    greeted = jnp.where(has_below, 1, 0) + jnp.where(has_above, 1, 0)
    pl.semaphore_wait(barrier, peers - 1 + greeted)

    def row_copy(step):
        target = (me + step) % peers
        return pltpu.make_async_remote_copy(
            src_ref=packed.at[target],
            dst_ref=arrived.at[step],
            send_sem=send_sem.at[step],
            recv_sem=recv_sem.at[step],
            device_id=(target, slab),
            device_id_type=MESH,
        )

    def start_rows(step, carry):
        row_copy(step).start()
        return carry

    lax.fori_loop(1, peers, start_rows, 0)

    depth = min(512, capacity)
    bundle = 8
    lane_cells = lax.broadcasted_iota(jnp.int32, (width, depth), 0).astype(jnp.float32)

    def clear(group, carry):
        total[group] = jnp.zeros((height, width), jnp.float32)
        return carry

    lax.fori_loop(0, groups, clear, 0)

    def add_rows(source, at):
        def part(index, carry):
            columns = pl.ds(pl.multiple_of(index * depth, depth), depth)
            block = source[at, :, columns]
            tags = block[comps // 16 * 16 :, :].astype(jnp.float32)
            low = tags[comps % 16 : comps % 16 + 1]
            high = tags[comps % 16 + 1 : comps % 16 + 2]
            match = jnp.where(lane_cells == low, 1.0, 0.0).astype(jnp.bfloat16)

            def product(group, inner):
                first = group * bundle
                masks = [
                    jnp.where(high == (first + n).astype(jnp.float32), 1.0, 0.0).astype(jnp.bfloat16)
                    for n in range(bundle)
                ]
                rows = jnp.concatenate([block * mask for mask in masks], axis=0)
                sums = lax.dot_general(rows, match, NT, preferred_element_type=jnp.float32)
                total[pl.ds(first, bundle)] += sums.reshape(bundle, height, width)
                return inner

            lax.fori_loop(0, groups // bundle, product, 0)
            return carry

        lax.fori_loop(0, capacity // depth, part, 0)

    add_rows(packed, me)

    def receive(step, carry):
        row_copy(step).wait_recv()
        add_rows(arrived, step)
        return carry

    lax.fori_loop(1, peers, receive, 0)

    def finish(group, carry):
        value = base[group].astype(jnp.float32) + total[group]
        updated[group % xcells, group // xcells] = value.astype(jnp.bfloat16)
        return carry

    lax.fori_loop(0, groups, finish, 0)

    def halo_copy(which, source, target, step):
        return pltpu.make_async_remote_copy(
            src_ref=source,
            dst_ref=target,
            send_sem=halo_send.at[which],
            recv_sem=halo_recv.at[which],
            device_id=((me + step + peers) % peers, slab),
            device_id_type=MESH,
        )

    to_next = halo_copy(0, updated.at[xcells - 1], left, 1)
    to_prev = halo_copy(1, updated.at[0], right, -1)
    face_to_prev = halo_copy(2, cx.at[0], next_cx, -1)

    @pl.when(has_next)
    def _():
        to_next.start()

    @pl.when(has_prev)
    def _():
        to_prev.start()
        face_to_prev.start()

    @pl.when(jnp.logical_not(has_prev))
    def _():
        left[...] = jnp.zeros_like(left)

    @pl.when(jnp.logical_not(has_next))
    def _():
        right[...] = jnp.zeros_like(right)
        next_cx[...] = jnp.zeros_like(next_cx)

    def flow_copy(i):
        return pltpu.make_async_remote_copy(
            src_ref=flow.at[i],
            dst_ref=inflow.at[i],
            send_sem=flow_send.at[i],
            recv_sem=flow_recv.at[i],
            device_id=(me, (slab + slabs - 1) % slabs),
            device_id_type=MESH,
        )

    reach = gain[0]
    for k in range(1, levels):
        reach = reach * gain[k]

    def advect(i):
        def level(counter, current_flow):
            k = levels - 1 - counter
            row = pl.ds(k, 1)
            current = updated[i, k].astype(jnp.float32)
            before = (left[k] if i == 0 else updated[i - 1, k]).astype(jnp.float32)
            after = (right[k] if i == xcells - 1 else updated[i + 1, k]).astype(jnp.float32)
            west = cx[i, row]
            east = next_cx[row] if i == xcells - 1 else cx[i + 1, row]
            south = cy[i, row]
            flux_west = jnp.maximum(west, 0.0) * before + jnp.minimum(west, 0.0) * current
            flux_east = jnp.maximum(east, 0.0) * current + jnp.minimum(east, 0.0) * after
            below = pltpu.roll(current, 1, 1)
            flux_south = jnp.maximum(south, 0.0) * below + jnp.minimum(south, 0.0) * current
            flux_north = pltpu.roll(flux_south, width - 1, 1)
            value = current - (flux_east - flux_west) - (flux_north - flux_south)
            value = value.astype(jnp.bfloat16)
            advected[i, k] = value
            return (value.astype(jnp.float32) + current_flow) * gain[k]

        flow[i] = lax.fori_loop(0, levels, level, jnp.zeros((height, width), jnp.float32))

    def chain(i):
        @pl.when(has_above)
        def _():
            flow_copy(i).wait_recv()
            flow[i] += reach * inflow[i]

        @pl.when(jnp.logical_not(has_above))
        def _():
            inflow[i] = jnp.zeros((height, width), jnp.float32)

        @pl.when(has_below)
        def _():
            flow_copy(i).start()

    for i in range(1, xcells - 1):
        advect(i)

    @pl.when(has_prev)
    def _():
        to_next.wait_recv()

    @pl.when(has_next)
    def _():
        to_prev.wait_recv()
        face_to_prev.wait_recv()

    for i in range(1, xcells - 1):
        chain(i)
    for i in (0, xcells - 1):
        advect(i)
        chain(i)

    for i in [*range(1, xcells - 1), 0, xcells - 1]:

        def settle(counter, current):
            k = levels - 1 - counter
            value = (advected[i, k].astype(jnp.float32) + current) * scale[k]
            out[k * xcells + i] = value.astype(jnp.bfloat16)
            return (advected[i, k].astype(jnp.float32) + current) * gain[k]

        lax.fori_loop(0, levels, settle, inflow[i])

    def sent(step, carry):
        row_copy(step).wait_send()
        return carry

    lax.fori_loop(1, peers, sent, 0)

    @pl.when(has_next)
    def _():
        to_next.wait_send()

    @pl.when(has_prev)
    def _():
        to_prev.wait_send()
        face_to_prev.wait_send()

    @pl.when(has_below)
    def _():
        for i in range(xcells):
            flow_copy(i).wait_send()


def per_device(base_field, increments, dest_tile, dest_cell, courant_x, courant_y, fall_courant):
    comps, levels, xcells, ycells = base_field.shape
    row_count = increments.shape[1]
    peers = lax.axis_size("xy")
    capacity = 2 * row_count // peers
    height = up(comps + 2, 16)
    groups = levels * xcells
    block = 512

    targets = dest_tile[:, 0]
    member = (targets[None, :] == jnp.arange(peers, dtype=jnp.int32)[:, None]).astype(jnp.int32)
    counts = running_counts(member)
    slots = targets * capacity + jnp.sum(counts * member, axis=0) - 1
    starts = jnp.pad(counts[:, block - 1 :: block], ((0, 0), (1, 0)))
    low = (dest_cell % ycells).astype(jnp.bfloat16)
    high = (dest_cell // ycells).astype(jnp.bfloat16)
    rows = jnp.concatenate(
        [
            increments,
            low[None],
            high[None],
            jnp.zeros((height - comps - 2, row_count), jnp.bfloat16),
        ],
        axis=0,
    )
    vmem = pl.BlockSpec(memory_space=pltpu.VMEM)
    packed = pl.pallas_call(
        functools.partial(pack_kernel, block),
        out_shape=jax.ShapeDtypeStruct((peers, height, capacity), jnp.bfloat16),
        in_specs=[pl.BlockSpec(memory_space=pltpu.SMEM), vmem, vmem],
        out_specs=vmem,
        compiler_params=pltpu.CompilerParams(vmem_limit_bytes=48 * 2**20),
        name="pack_rows",
    )(starts, rows, slots[None])

    pad_comps = ((0, 0), (0, height - comps), (0, 0))
    base = jnp.pad(
        jnp.transpose(base_field, (1, 2, 0, 3)).reshape(groups, comps, ycells), pad_comps
    )
    first = jnp.logical_and(
        lax.axis_index("xy") == 0, jnp.arange(xcells)[:, None, None] == 0
    )
    face_x = jnp.where(first, 0.0, jnp.transpose(courant_x.astype(jnp.float32), (1, 0, 2)))
    face_y = jnp.transpose(courant_y.astype(jnp.float32), (1, 0, 2))
    face_y = jnp.where(jnp.arange(ycells)[None, None, :] == 0, 0.0, face_y)
    fall = lax.dynamic_slice_in_dim(fall_courant, lax.axis_index("gz") * levels, levels, 1)
    fall = jnp.pad(jnp.transpose(fall)[:, :, None], pad_comps)
    scale = 1.0 / (1.0 + fall)
    gain = fall / (1.0 + fall)

    settled = pl.pallas_call(
        functools.partial(main_kernel, comps),
        out_shape=jax.ShapeDtypeStruct((groups, height, ycells), jnp.bfloat16),
        in_specs=[vmem] * 6,
        out_specs=vmem,
        scratch_shapes=[
            pltpu.VMEM((peers, height, capacity), jnp.bfloat16),
            pltpu.VMEM((groups, height, ycells), jnp.float32),
            pltpu.VMEM((xcells, levels, height, ycells), jnp.bfloat16),
            pltpu.VMEM((xcells, levels, height, ycells), jnp.bfloat16),
            pltpu.VMEM((levels, height, ycells), jnp.bfloat16),
            pltpu.VMEM((levels, height, ycells), jnp.bfloat16),
            pltpu.VMEM((levels, ycells), jnp.float32),
            pltpu.VMEM((xcells, height, ycells), jnp.float32),
            pltpu.VMEM((xcells, height, ycells), jnp.float32),
            pltpu.SemaphoreType.DMA((peers,)),
            pltpu.SemaphoreType.DMA((peers,)),
            pltpu.SemaphoreType.DMA((3,)),
            pltpu.SemaphoreType.DMA((3,)),
            pltpu.SemaphoreType.DMA((xcells,)),
            pltpu.SemaphoreType.DMA((xcells,)),
        ],
        compiler_params=pltpu.CompilerParams(
            vmem_limit_bytes=56 * 2**20, collective_id=0, has_side_effects=True
        ),
        name="exchange_advect_settle",
    )(packed, base, face_x, face_y, scale, gain)
    settled = settled.reshape(levels, xcells, height, ycells)[:, :, :comps]
    return jnp.transpose(settled, (2, 0, 1, 3))


def solution(mesh):
    in_specs = (
        P(None, "gz", "xy", None),
        P(None, ("xy", "gz")),
        P(("xy", "gz"), None),
        P(("xy", "gz")),
        P("gz", "xy", None),
        P("gz", "xy", None),
        P(),
    )
    out_specs = P(None, "gz", "xy", None)
    return jax.shard_map(
        per_device, mesh=mesh, in_specs=in_specs, out_specs=out_specs, check_vma=False
    )
```

```python
import functools

import jax
import jax.numpy as jnp
from jax import lax
from jax.experimental import pallas as pl
from jax.experimental.pallas import tpu as pltpu
from jax.sharding import PartitionSpec as P

MESH = pl.DeviceIdType.MESH
NT = (((1,), (1,)), ((), ()))


def up(value, multiple):
    return -(-value // multiple) * multiple


def running_counts(member):
    tiles, count = member.shape
    run = 128
    grouped = member.astype(jnp.bfloat16).reshape(tiles * (count // run), run)
    inside = jnp.dot(
        grouped, jnp.triu(jnp.ones((run, run), jnp.bfloat16)), preferred_element_type=jnp.float32
    ).reshape(tiles, count // run, run)
    before = jnp.dot(
        inside[:, :, run - 1].astype(jnp.bfloat16),
        jnp.triu(jnp.ones((count // run, count // run), jnp.bfloat16), 1),
        preferred_element_type=jnp.float32,
    )
    return (inside + before[:, :, None]).reshape(tiles, count).astype(jnp.int32)


def pack_kernel(block, starts_ref, rows_ref, slot_ref, out_ref):
    peers, height, capacity = out_ref.shape
    width = min(256, capacity)
    blocks = rows_ref.shape[1] // block
    window = lax.broadcasted_iota(jnp.int32, (width, block), 0)

    def clear(tile, carry):
        out_ref[tile] = jnp.zeros((height, capacity), out_ref.dtype)
        return carry

    lax.fori_loop(0, peers, clear, 0)

    bundle = min(8, peers)
    windows = capacity // width

    def step(counter, carry):
        part, first_tile = counter // (peers // bundle), counter % (peers // bundle) * bundle
        columns = pl.ds(pl.multiple_of(part * block, block), block)
        slots = slot_ref[:, columns]

        def match(tile, chunk):
            base = tile * capacity + chunk * width
            return jnp.where(window == slots - base, 1.0, 0.0).astype(jnp.bfloat16)

        def move(matches):
            return lax.dot_general(
                rows_ref[:, columns], matches, NT, preferred_element_type=jnp.float32
            ).astype(out_ref.dtype)

        def spot(chunk):
            return pl.ds(pl.multiple_of(chunk * width, width), width)

        tiles = [first_tile + n for n in range(bundle)]
        chunks = [jnp.minimum(starts_ref[tile, part] // width, windows - 1) for tile in tiles]
        moved = move(jnp.concatenate([match(*pair) for pair in zip(tiles, chunks)], axis=0))
        for n in range(bundle):
            out_ref[tiles[n], :, spot(chunks[n])] += moved[:, n * width : (n + 1) * width]

        def more(tile, inner):
            start = starts_ref[tile, part]
            stop = starts_ref[tile, part + 1]

            def place(chunk, innermost):
                out_ref[tile, :, spot(chunk)] += move(match(tile, chunk))
                return innermost

            lax.fori_loop(start // width + 1, (stop + width - 1) // width, place, 0)
            return inner

        lax.fori_loop(first_tile, first_tile + bundle, more, 0)
        return carry

    lax.fori_loop(0, blocks * (peers // bundle), step, 0)


def main_kernel(
    comps, packed, base, cx, cy, scale, gain, out, arrived, total, updated, advected, left, right,
    next_cx, flow, inflow, send_sem, recv_sem, halo_send, halo_recv, flow_send, flow_recv,
):
    peers, height, capacity = packed.shape
    xcells, levels, _, width = updated.shape
    slabs = lax.axis_size("gz")
    me, slab = lax.axis_index("xy"), lax.axis_index("gz")
    has_prev, has_next = me > 0, me < peers - 1
    has_below, has_above = slab > 0, slab < slabs - 1
    groups = xcells * levels

    barrier = pltpu.get_barrier_semaphore()

    def greet(step, carry):
        pl.semaphore_signal(
            barrier, inc=1, device_id=((me + step) % peers, slab), device_id_type=MESH
        )
        return carry

    lax.fori_loop(1, peers, greet, 0)

    @pl.when(has_below)
    def _():
        pl.semaphore_signal(barrier, inc=1, device_id=(me, slab - 1), device_id_type=MESH)

    @pl.when(has_above)
    def _():
        pl.semaphore_signal(barrier, inc=1, device_id=(me, slab + 1), device_id_type=MESH)

    greeted = jnp.where(has_below, 1, 0) + jnp.where(has_above, 1, 0)
    pl.semaphore_wait(barrier, peers - 1 + greeted)

    def row_copy(step):
        target = (me + step) % peers
        return pltpu.make_async_remote_copy(
            src_ref=packed.at[target],
            dst_ref=arrived.at[step],
            send_sem=send_sem.at[step],
            recv_sem=recv_sem.at[step],
            device_id=(target, slab),
            device_id_type=MESH,
        )

    def start_rows(step, carry):
        row_copy(step).start()
        return carry

    lax.fori_loop(1, peers, start_rows, 0)

    depth = min(512, capacity)
    bundle = 8
    lane_cells = lax.broadcasted_iota(jnp.int32, (width, depth), 0).astype(jnp.float32)

    def clear(group, carry):
        total[group] = jnp.zeros((height, width), jnp.float32)
        tail = comps // 16 * 16
        updated[group % xcells, group // xcells, tail:, :] = jnp.zeros(
            (height - tail, width), jnp.bfloat16
        )
        return carry

    lax.fori_loop(0, groups, clear, 0)

    def add_rows(source, at):
        def part(index, carry):
            columns = pl.ds(pl.multiple_of(index * depth, depth), depth)
            block = source[at, :, columns]
            tags = block[comps // 16 * 16 :, :].astype(jnp.float32)
            low = tags[comps % 16 : comps % 16 + 1]
            high = tags[comps % 16 + 1 : comps % 16 + 2]
            match = jnp.where(lane_cells == low, 1.0, 0.0).astype(jnp.bfloat16)

            def product(group, inner):
                first = group * bundle
                masks = [
                    jnp.where(high == (first + n).astype(jnp.float32), 1.0, 0.0).astype(jnp.bfloat16)
                    for n in range(bundle)
                ]
                rows = jnp.concatenate([block * mask for mask in masks], axis=0)
                sums = lax.dot_general(rows, match, NT, preferred_element_type=jnp.float32)
                total[pl.ds(first, bundle)] += sums.reshape(bundle, height, width)
                return inner

            lax.fori_loop(0, groups // bundle, product, 0)
            return carry

        lax.fori_loop(0, capacity // depth, part, 0)

    add_rows(packed, me)

    def receive(step, carry):
        row_copy(step).wait_recv()
        add_rows(arrived, step)
        return carry

    lax.fori_loop(1, peers, receive, 0)

    def finish(group, carry):
        value = base[group].astype(jnp.float32) + total[group, :comps]
        updated[group % xcells, group // xcells, :comps] = value.astype(jnp.bfloat16)
        return carry

    lax.fori_loop(0, groups, finish, 0)

    def halo_copy(which, source, target, step):
        return pltpu.make_async_remote_copy(
            src_ref=source,
            dst_ref=target,
            send_sem=halo_send.at[which],
            recv_sem=halo_recv.at[which],
            device_id=((me + step + peers) % peers, slab),
            device_id_type=MESH,
        )

    to_next = halo_copy(0, updated.at[xcells - 1], left, 1)
    to_prev = halo_copy(1, updated.at[0], right, -1)
    face_to_prev = halo_copy(2, cx.at[0], next_cx, -1)

    @pl.when(has_next)
    def _():
        to_next.start()

    @pl.when(has_prev)
    def _():
        to_prev.start()
        face_to_prev.start()

    @pl.when(jnp.logical_not(has_prev))
    def _():
        left[...] = jnp.zeros_like(left)

    @pl.when(jnp.logical_not(has_next))
    def _():
        right[...] = jnp.zeros_like(right)
        next_cx[...] = jnp.zeros_like(next_cx)

    def flow_copy(i):
        return pltpu.make_async_remote_copy(
            src_ref=flow.at[i],
            dst_ref=inflow.at[i],
            send_sem=flow_send.at[i],
            recv_sem=flow_recv.at[i],
            device_id=(me, (slab + slabs - 1) % slabs),
            device_id_type=MESH,
        )

    reach = gain[0]
    for k in range(1, levels):
        reach = reach * gain[k]

    def advect(i):
        def level(counter, current_flow):
            k = levels - 1 - counter
            row = pl.ds(k, 1)
            current = updated[i, k].astype(jnp.float32)
            before = (left[k] if i == 0 else updated[i - 1, k]).astype(jnp.float32)
            after = (right[k] if i == xcells - 1 else updated[i + 1, k]).astype(jnp.float32)
            west = cx[i, row]
            east = next_cx[row] if i == xcells - 1 else cx[i + 1, row]
            south = cy[i, row]
            flux_west = jnp.maximum(west, 0.0) * before + jnp.minimum(west, 0.0) * current
            flux_east = jnp.maximum(east, 0.0) * current + jnp.minimum(east, 0.0) * after
            below = pltpu.roll(current, 1, 1)
            flux_south = jnp.maximum(south, 0.0) * below + jnp.minimum(south, 0.0) * current
            flux_north = pltpu.roll(flux_south, width - 1, 1)
            value = current - (flux_east - flux_west) - (flux_north - flux_south)
            value = value.astype(jnp.bfloat16)
            advected[i, k] = value
            return (value.astype(jnp.float32) + current_flow) * gain[k]

        flow[i] = lax.fori_loop(0, levels, level, jnp.zeros((height, width), jnp.float32))

    def chain(i):
        @pl.when(has_above)
        def _():
            flow_copy(i).wait_recv()
            flow[i] += reach * inflow[i]

        @pl.when(jnp.logical_not(has_above))
        def _():
            inflow[i] = jnp.zeros((height, width), jnp.float32)

        @pl.when(has_below)
        def _():
            flow_copy(i).start()

    for i in range(1, xcells - 1):
        advect(i)

    @pl.when(has_prev)
    def _():
        to_next.wait_recv()

    @pl.when(has_next)
    def _():
        to_prev.wait_recv()
        face_to_prev.wait_recv()

    for i in range(1, xcells - 1):
        chain(i)
    for i in (0, xcells - 1):
        advect(i)
        chain(i)

    for i in [*range(1, xcells - 1), 0, xcells - 1]:

        def settle(counter, current):
            k = levels - 1 - counter
            value = (advected[i, k].astype(jnp.float32) + current) * scale[k]
            out[k * xcells + i] = value[:comps].astype(jnp.bfloat16)
            return (advected[i, k].astype(jnp.float32) + current) * gain[k]

        lax.fori_loop(0, levels, settle, inflow[i])

    def sent(step, carry):
        row_copy(step).wait_send()
        return carry

    lax.fori_loop(1, peers, sent, 0)

    @pl.when(has_next)
    def _():
        to_next.wait_send()

    @pl.when(has_prev)
    def _():
        to_prev.wait_send()
        face_to_prev.wait_send()

    @pl.when(has_below)
    def _():
        for i in range(xcells):
            flow_copy(i).wait_send()


def per_device(base_field, increments, dest_tile, dest_cell, courant_x, courant_y, fall_courant):
    comps, levels, xcells, ycells = base_field.shape
    row_count = increments.shape[1]
    peers = lax.axis_size("xy")
    capacity = 2 * row_count // peers
    height = up(comps + 2, 16)
    groups = levels * xcells
    block = 512

    targets = dest_tile[:, 0]
    member = (targets[None, :] == jnp.arange(peers, dtype=jnp.int32)[:, None]).astype(jnp.int32)
    counts = running_counts(member)
    slots = targets * capacity + jnp.sum(counts * member, axis=0) - 1
    starts = jnp.pad(counts[:, block - 1 :: block], ((0, 0), (1, 0)))
    low = (dest_cell % ycells).astype(jnp.bfloat16)
    high = (dest_cell // ycells).astype(jnp.bfloat16)
    rows = jnp.concatenate(
        [
            increments,
            low[None],
            high[None],
            jnp.zeros((height - comps - 2, row_count), jnp.bfloat16),
        ],
        axis=0,
    )
    vmem = pl.BlockSpec(memory_space=pltpu.VMEM)
    packed = pl.pallas_call(
        functools.partial(pack_kernel, block),
        out_shape=jax.ShapeDtypeStruct((peers, height, capacity), jnp.bfloat16),
        in_specs=[pl.BlockSpec(memory_space=pltpu.SMEM), vmem, vmem],
        out_specs=vmem,
        compiler_params=pltpu.CompilerParams(vmem_limit_bytes=48 * 2**20),
        name="pack_rows",
    )(starts, rows, slots[None])

    pad_comps = ((0, 0), (0, height - comps), (0, 0))
    base = jnp.transpose(base_field, (1, 2, 0, 3)).reshape(groups, comps, ycells)
    first = jnp.logical_and(
        lax.axis_index("xy") == 0, jnp.arange(xcells)[:, None, None] == 0
    )
    face_x = jnp.where(first, 0.0, jnp.transpose(courant_x.astype(jnp.float32), (1, 0, 2)))
    face_y = jnp.transpose(courant_y.astype(jnp.float32), (1, 0, 2))
    face_y = jnp.where(jnp.arange(ycells)[None, None, :] == 0, 0.0, face_y)
    fall = lax.dynamic_slice_in_dim(fall_courant, lax.axis_index("gz") * levels, levels, 1)
    fall = jnp.pad(jnp.transpose(fall)[:, :, None], pad_comps)
    scale = 1.0 / (1.0 + fall)
    gain = fall / (1.0 + fall)

    settled = pl.pallas_call(
        functools.partial(main_kernel, comps),
        out_shape=jax.ShapeDtypeStruct((groups, comps, ycells), jnp.bfloat16),
        in_specs=[vmem] * 6,
        out_specs=vmem,
        scratch_shapes=[
            pltpu.VMEM((peers, height, capacity), jnp.bfloat16),
            pltpu.VMEM((groups, height, ycells), jnp.float32),
            pltpu.VMEM((xcells, levels, height, ycells), jnp.bfloat16),
            pltpu.VMEM((xcells, levels, height, ycells), jnp.bfloat16),
            pltpu.VMEM((levels, height, ycells), jnp.bfloat16),
            pltpu.VMEM((levels, height, ycells), jnp.bfloat16),
            pltpu.VMEM((levels, ycells), jnp.float32),
            pltpu.VMEM((xcells, height, ycells), jnp.float32),
            pltpu.VMEM((xcells, height, ycells), jnp.float32),
            pltpu.SemaphoreType.DMA((peers,)),
            pltpu.SemaphoreType.DMA((peers,)),
            pltpu.SemaphoreType.DMA((3,)),
            pltpu.SemaphoreType.DMA((3,)),
            pltpu.SemaphoreType.DMA((xcells,)),
            pltpu.SemaphoreType.DMA((xcells,)),
        ],
        compiler_params=pltpu.CompilerParams(
            vmem_limit_bytes=56 * 2**20, collective_id=0, has_side_effects=True
        ),
        name="exchange_advect_settle",
    )(packed, base, face_x, face_y, scale, gain)
    settled = settled.reshape(levels, xcells, comps, ycells)
    return jnp.transpose(settled, (2, 0, 1, 3))


def solution(mesh):
    in_specs = (
        P(None, "gz", "xy", None),
        P(None, ("xy", "gz")),
        P(("xy", "gz"), None),
        P(("xy", "gz")),
        P("gz", "xy", None),
        P("gz", "xy", None),
        P(),
    )
    out_specs = P(None, "gz", "xy", None)
    return jax.shard_map(
        per_device, mesh=mesh, in_specs=in_specs, out_specs=out_specs, check_vma=False
    )
```

```python
import functools

import jax
import jax.numpy as jnp
from jax import lax
from jax.experimental import pallas as pl
from jax.experimental.pallas import tpu as pltpu
from jax.sharding import PartitionSpec as P

MESH = pl.DeviceIdType.MESH
NT = (((1,), (1,)), ((), ()))


def up(value, multiple):
    return -(-value // multiple) * multiple


def running_counts(member):
    tiles, count = member.shape
    run = 128
    grouped = member.astype(jnp.bfloat16).reshape(tiles * (count // run), run)
    inside = jnp.dot(
        grouped, jnp.triu(jnp.ones((run, run), jnp.bfloat16)), preferred_element_type=jnp.float32
    ).reshape(tiles, count // run, run)
    before = jnp.dot(
        inside[:, :, run - 1].astype(jnp.bfloat16),
        jnp.triu(jnp.ones((count // run, count // run), jnp.bfloat16), 1),
        preferred_element_type=jnp.float32,
    )
    return (inside + before[:, :, None]).reshape(tiles, count).astype(jnp.int32)


def pack_kernel(block, starts_ref, rows_ref, slot_ref, out_ref):
    peers, height, capacity = out_ref.shape
    width = min(256, capacity)
    blocks = rows_ref.shape[1] // block
    window = lax.broadcasted_iota(jnp.int32, (width, block), 0)

    def clear(tile, carry):
        out_ref[tile] = jnp.zeros((height, capacity), out_ref.dtype)
        return carry

    lax.fori_loop(0, peers, clear, 0)

    bundle = min(8, peers)
    windows = capacity // width

    def step(counter, carry):
        part, first_tile = counter // (peers // bundle), counter % (peers // bundle) * bundle
        columns = pl.ds(pl.multiple_of(part * block, block), block)
        slots = slot_ref[:, columns]

        def match(tile, chunk):
            base = tile * capacity + chunk * width
            return jnp.where(window == slots - base, 1.0, 0.0).astype(jnp.bfloat16)

        def move(matches):
            return lax.dot_general(
                rows_ref[:, columns], matches, NT, preferred_element_type=jnp.float32
            ).astype(out_ref.dtype)

        def spot(chunk):
            return pl.ds(pl.multiple_of(chunk * width, width), width)

        tiles = [first_tile + n for n in range(bundle)]
        chunks = [jnp.minimum(starts_ref[tile, part] // width, windows - 1) for tile in tiles]
        moved = move(jnp.concatenate([match(*pair) for pair in zip(tiles, chunks)], axis=0))
        for n in range(bundle):
            out_ref[tiles[n], :, spot(chunks[n])] += moved[:, n * width : (n + 1) * width]

        def more(tile, inner):
            start = starts_ref[tile, part]
            stop = starts_ref[tile, part + 1]

            def place(chunk, innermost):
                out_ref[tile, :, spot(chunk)] += move(match(tile, chunk))
                return innermost

            lax.fori_loop(start // width + 1, (stop + width - 1) // width, place, 0)
            return inner

        lax.fori_loop(first_tile, first_tile + bundle, more, 0)
        return carry

    lax.fori_loop(0, blocks * (peers // bundle), step, 0)


def main_kernel(
    comps, packed, base, cx, cy, scale, gain, out, arrived, total, updated, advected, left, right,
    next_cx, flow, inflow, send_sem, recv_sem, halo_send, halo_recv, flow_send, flow_recv,
):
    peers, height, capacity = packed.shape
    xcells, levels, _, width = updated.shape
    slabs = lax.axis_size("gz")
    me, slab = lax.axis_index("xy"), lax.axis_index("gz")
    has_prev, has_next = me > 0, me < peers - 1
    has_below, has_above = slab > 0, slab < slabs - 1
    groups = xcells * levels

    barrier = pltpu.get_barrier_semaphore()

    def greet(step, carry):
        pl.semaphore_signal(
            barrier, inc=1, device_id=((me + step) % peers, slab), device_id_type=MESH
        )
        return carry

    lax.fori_loop(1, peers, greet, 0)

    @pl.when(has_below)
    def _():
        pl.semaphore_signal(barrier, inc=1, device_id=(me, slab - 1), device_id_type=MESH)

    @pl.when(has_above)
    def _():
        pl.semaphore_signal(barrier, inc=1, device_id=(me, slab + 1), device_id_type=MESH)

    greeted = jnp.where(has_below, 1, 0) + jnp.where(has_above, 1, 0)
    pl.semaphore_wait(barrier, peers - 1 + greeted)

    def row_copy(step):
        target = (me + step) % peers
        return pltpu.make_async_remote_copy(
            src_ref=packed.at[target],
            dst_ref=arrived.at[step],
            send_sem=send_sem.at[step],
            recv_sem=recv_sem.at[step],
            device_id=(target, slab),
            device_id_type=MESH,
        )

    def start_rows(step, carry):
        row_copy(step).start()
        return carry

    lax.fori_loop(1, peers, start_rows, 0)

    depth = min(1024, capacity)
    bundle = 8
    lane_cells = lax.broadcasted_iota(jnp.int32, (width, depth), 0).astype(jnp.float32)

    def clear(group, carry):
        total[group] = jnp.zeros((height, width), jnp.float32)
        tail = comps // 16 * 16
        updated[group % xcells, group // xcells, tail:, :] = jnp.zeros(
            (height - tail, width), jnp.bfloat16
        )
        return carry

    lax.fori_loop(0, groups, clear, 0)

    def add_rows(source, at):
        def part(index, carry):
            columns = pl.ds(pl.multiple_of(index * depth, depth), depth)
            block = source[at, :, columns]
            tags = block[comps // 16 * 16 :, :].astype(jnp.float32)
            low = tags[comps % 16 : comps % 16 + 1]
            high = tags[comps % 16 + 1 : comps % 16 + 2]
            match = jnp.where(lane_cells == low, 1.0, 0.0).astype(jnp.bfloat16)

            def product(group, inner):
                first = group * bundle
                masks = [
                    jnp.where(high == (first + n).astype(jnp.float32), 1.0, 0.0).astype(jnp.bfloat16)
                    for n in range(bundle)
                ]
                rows = jnp.concatenate([block * mask for mask in masks], axis=0)
                sums = lax.dot_general(rows, match, NT, preferred_element_type=jnp.float32)
                total[pl.ds(first, bundle)] += sums.reshape(bundle, height, width)
                return inner

            lax.fori_loop(0, groups // bundle, product, 0)
            return carry

        lax.fori_loop(0, capacity // depth, part, 0)

    add_rows(packed, me)

    def receive(step, carry):
        row_copy(step).wait_recv()
        add_rows(arrived, step)
        return carry

    lax.fori_loop(1, peers, receive, 0)

    def finish(group, carry):
        value = base[group].astype(jnp.float32) + total[group, :comps]
        updated[group % xcells, group // xcells, :comps] = value.astype(jnp.bfloat16)
        return carry

    lax.fori_loop(0, groups, finish, 0)

    def halo_copy(which, source, target, step):
        return pltpu.make_async_remote_copy(
            src_ref=source,
            dst_ref=target,
            send_sem=halo_send.at[which],
            recv_sem=halo_recv.at[which],
            device_id=((me + step + peers) % peers, slab),
            device_id_type=MESH,
        )

    to_next = halo_copy(0, updated.at[xcells - 1], left, 1)
    to_prev = halo_copy(1, updated.at[0], right, -1)
    face_to_prev = halo_copy(2, cx.at[0], next_cx, -1)

    @pl.when(has_next)
    def _():
        to_next.start()

    @pl.when(has_prev)
    def _():
        to_prev.start()
        face_to_prev.start()

    @pl.when(jnp.logical_not(has_prev))
    def _():
        left[...] = jnp.zeros_like(left)

    @pl.when(jnp.logical_not(has_next))
    def _():
        right[...] = jnp.zeros_like(right)
        next_cx[...] = jnp.zeros_like(next_cx)

    def flow_copy(i):
        return pltpu.make_async_remote_copy(
            src_ref=flow.at[i],
            dst_ref=inflow.at[i],
            send_sem=flow_send.at[i],
            recv_sem=flow_recv.at[i],
            device_id=(me, (slab + slabs - 1) % slabs),
            device_id_type=MESH,
        )

    reach = gain[0]
    for k in range(1, levels):
        reach = reach * gain[k]

    def advect(i):
        def level(counter, current_flow):
            k = levels - 1 - counter
            row = pl.ds(k, 1)
            current = updated[i, k].astype(jnp.float32)
            before = (left[k] if i == 0 else updated[i - 1, k]).astype(jnp.float32)
            after = (right[k] if i == xcells - 1 else updated[i + 1, k]).astype(jnp.float32)
            west = cx[i, row]
            east = next_cx[row] if i == xcells - 1 else cx[i + 1, row]
            south = cy[i, row]
            flux_west = jnp.maximum(west, 0.0) * before + jnp.minimum(west, 0.0) * current
            flux_east = jnp.maximum(east, 0.0) * current + jnp.minimum(east, 0.0) * after
            below = pltpu.roll(current, 1, 1)
            flux_south = jnp.maximum(south, 0.0) * below + jnp.minimum(south, 0.0) * current
            flux_north = pltpu.roll(flux_south, width - 1, 1)
            value = current - (flux_east - flux_west) - (flux_north - flux_south)
            value = value.astype(jnp.bfloat16)
            advected[i, k] = value
            return (value.astype(jnp.float32) + current_flow) * gain[k]

        flow[i] = lax.fori_loop(0, levels, level, jnp.zeros((height, width), jnp.float32))

    def chain(i):
        @pl.when(has_above)
        def _():
            flow_copy(i).wait_recv()
            flow[i] += reach * inflow[i]

        @pl.when(jnp.logical_not(has_above))
        def _():
            inflow[i] = jnp.zeros((height, width), jnp.float32)

        @pl.when(has_below)
        def _():
            flow_copy(i).start()

    for i in range(1, xcells - 1):
        advect(i)

    @pl.when(has_prev)
    def _():
        to_next.wait_recv()

    @pl.when(has_next)
    def _():
        to_prev.wait_recv()
        face_to_prev.wait_recv()

    for i in range(1, xcells - 1):
        chain(i)
    for i in (0, xcells - 1):
        advect(i)
        chain(i)

    for i in [*range(1, xcells - 1), 0, xcells - 1]:

        def settle(counter, current):
            k = levels - 1 - counter
            value = (advected[i, k].astype(jnp.float32) + current) * scale[k]
            out[k * xcells + i] = value[:comps].astype(jnp.bfloat16)
            return (advected[i, k].astype(jnp.float32) + current) * gain[k]

        lax.fori_loop(0, levels, settle, inflow[i])

    def sent(step, carry):
        row_copy(step).wait_send()
        return carry

    lax.fori_loop(1, peers, sent, 0)

    @pl.when(has_next)
    def _():
        to_next.wait_send()

    @pl.when(has_prev)
    def _():
        to_prev.wait_send()
        face_to_prev.wait_send()

    @pl.when(has_below)
    def _():
        for i in range(xcells):
            flow_copy(i).wait_send()


def per_device(base_field, increments, dest_tile, dest_cell, courant_x, courant_y, fall_courant):
    comps, levels, xcells, ycells = base_field.shape
    row_count = increments.shape[1]
    peers = lax.axis_size("xy")
    capacity = 2 * row_count // peers
    height = up(comps + 2, 16)
    groups = levels * xcells
    block = 512

    targets = dest_tile[:, 0]
    member = (targets[None, :] == jnp.arange(peers, dtype=jnp.int32)[:, None]).astype(jnp.int32)
    counts = running_counts(member)
    slots = targets * capacity + jnp.sum(counts * member, axis=0) - 1
    starts = jnp.pad(counts[:, block - 1 :: block], ((0, 0), (1, 0)))
    low = (dest_cell % ycells).astype(jnp.bfloat16)
    high = (dest_cell // ycells).astype(jnp.bfloat16)
    rows = jnp.concatenate(
        [
            increments,
            low[None],
            high[None],
            jnp.zeros((height - comps - 2, row_count), jnp.bfloat16),
        ],
        axis=0,
    )
    vmem = pl.BlockSpec(memory_space=pltpu.VMEM)
    packed = pl.pallas_call(
        functools.partial(pack_kernel, block),
        out_shape=jax.ShapeDtypeStruct((peers, height, capacity), jnp.bfloat16),
        in_specs=[pl.BlockSpec(memory_space=pltpu.SMEM), vmem, vmem],
        out_specs=vmem,
        compiler_params=pltpu.CompilerParams(vmem_limit_bytes=48 * 2**20),
        name="pack_rows",
    )(starts, rows, slots[None])

    pad_comps = ((0, 0), (0, height - comps), (0, 0))
    base = jnp.transpose(base_field, (1, 2, 0, 3)).reshape(groups, comps, ycells)
    first = jnp.logical_and(
        lax.axis_index("xy") == 0, jnp.arange(xcells)[:, None, None] == 0
    )
    face_x = jnp.where(first, 0.0, jnp.transpose(courant_x.astype(jnp.float32), (1, 0, 2)))
    face_y = jnp.transpose(courant_y.astype(jnp.float32), (1, 0, 2))
    face_y = jnp.where(jnp.arange(ycells)[None, None, :] == 0, 0.0, face_y)
    fall = lax.dynamic_slice_in_dim(fall_courant, lax.axis_index("gz") * levels, levels, 1)
    fall = jnp.pad(jnp.transpose(fall)[:, :, None], pad_comps)
    scale = 1.0 / (1.0 + fall)
    gain = fall / (1.0 + fall)

    settled = pl.pallas_call(
        functools.partial(main_kernel, comps),
        out_shape=jax.ShapeDtypeStruct((groups, comps, ycells), jnp.bfloat16),
        in_specs=[vmem] * 6,
        out_specs=vmem,
        scratch_shapes=[
            pltpu.VMEM((peers, height, capacity), jnp.bfloat16),
            pltpu.VMEM((groups, height, ycells), jnp.float32),
            pltpu.VMEM((xcells, levels, height, ycells), jnp.bfloat16),
            pltpu.VMEM((xcells, levels, height, ycells), jnp.bfloat16),
            pltpu.VMEM((levels, height, ycells), jnp.bfloat16),
            pltpu.VMEM((levels, height, ycells), jnp.bfloat16),
            pltpu.VMEM((levels, ycells), jnp.float32),
            pltpu.VMEM((xcells, height, ycells), jnp.float32),
            pltpu.VMEM((xcells, height, ycells), jnp.float32),
            pltpu.SemaphoreType.DMA((peers,)),
            pltpu.SemaphoreType.DMA((peers,)),
            pltpu.SemaphoreType.DMA((3,)),
            pltpu.SemaphoreType.DMA((3,)),
            pltpu.SemaphoreType.DMA((xcells,)),
            pltpu.SemaphoreType.DMA((xcells,)),
        ],
        compiler_params=pltpu.CompilerParams(
            vmem_limit_bytes=56 * 2**20, collective_id=0, has_side_effects=True
        ),
        name="exchange_advect_settle",
    )(packed, base, face_x, face_y, scale, gain)
    settled = settled.reshape(levels, xcells, comps, ycells)
    return jnp.transpose(settled, (2, 0, 1, 3))


def solution(mesh):
    in_specs = (
        P(None, "gz", "xy", None),
        P(None, ("xy", "gz")),
        P(("xy", "gz"), None),
        P(("xy", "gz")),
        P("gz", "xy", None),
        P("gz", "xy", None),
        P(),
    )
    out_specs = P(None, "gz", "xy", None)
    return jax.shard_map(
        per_device, mesh=mesh, in_specs=in_specs, out_specs=out_specs, check_vma=False
    )
```

```python
import functools

import jax
import jax.numpy as jnp
from jax import lax
from jax.experimental import pallas as pl
from jax.experimental.pallas import tpu as pltpu
from jax.sharding import PartitionSpec as P

MESH = pl.DeviceIdType.MESH
NT = (((1,), (1,)), ((), ()))


def up(value, multiple):
    return -(-value // multiple) * multiple


def running_counts(member):
    tiles, count = member.shape
    run = 128
    grouped = member.astype(jnp.bfloat16).reshape(tiles * (count // run), run)
    inside = jnp.dot(
        grouped, jnp.triu(jnp.ones((run, run), jnp.bfloat16)), preferred_element_type=jnp.float32
    ).reshape(tiles, count // run, run)
    before = jnp.dot(
        inside[:, :, run - 1].astype(jnp.bfloat16),
        jnp.triu(jnp.ones((count // run, count // run), jnp.bfloat16), 1),
        preferred_element_type=jnp.float32,
    )
    return (inside + before[:, :, None]).reshape(tiles, count).astype(jnp.int32)


def pack_kernel(block, starts_ref, rows_ref, slot_ref, out_ref):
    peers, height, capacity = out_ref.shape
    width = min(256, capacity)
    blocks = rows_ref.shape[1] // block
    window = lax.broadcasted_iota(jnp.int32, (width, block), 0)

    def clear(tile, carry):
        out_ref[tile] = jnp.zeros((height, capacity), out_ref.dtype)
        return carry

    lax.fori_loop(0, peers, clear, 0)

    bundle = min(8, peers)
    windows = capacity // width

    def step(counter, carry):
        part, first_tile = counter // (peers // bundle), counter % (peers // bundle) * bundle
        columns = pl.ds(pl.multiple_of(part * block, block), block)
        slots = slot_ref[:, columns]

        def match(tile, chunk):
            base = tile * capacity + chunk * width
            return jnp.where(window == slots - base, 1.0, 0.0).astype(jnp.bfloat16)

        def move(matches):
            return lax.dot_general(
                rows_ref[:, columns], matches, NT, preferred_element_type=jnp.float32
            ).astype(out_ref.dtype)

        def spot(chunk):
            return pl.ds(pl.multiple_of(chunk * width, width), width)

        tiles = [first_tile + n for n in range(bundle)]
        chunks = [jnp.minimum(starts_ref[tile, part] // width, windows - 1) for tile in tiles]
        moved = move(jnp.concatenate([match(*pair) for pair in zip(tiles, chunks)], axis=0))
        for n in range(bundle):
            out_ref[tiles[n], :, spot(chunks[n])] += moved[:, n * width : (n + 1) * width]

        def more(tile, inner):
            start = starts_ref[tile, part]
            stop = starts_ref[tile, part + 1]

            def place(chunk, innermost):
                out_ref[tile, :, spot(chunk)] += move(match(tile, chunk))
                return innermost

            lax.fori_loop(start // width + 1, (stop + width - 1) // width, place, 0)
            return inner

        lax.fori_loop(first_tile, first_tile + bundle, more, 0)
        return carry

    lax.fori_loop(0, blocks * (peers // bundle), step, 0)


def main_kernel(
    comps, packed, base, cx, cy, scale, gain, out, arrived, total, updated, advected, left, right,
    next_cx, flow, inflow, send_sem, recv_sem, halo_send, halo_recv, flow_send, flow_recv,
):
    peers, height, capacity = packed.shape
    xcells, levels, _, width = updated.shape
    slabs = lax.axis_size("gz")
    me, slab = lax.axis_index("xy"), lax.axis_index("gz")
    has_prev, has_next = me > 0, me < peers - 1
    has_below, has_above = slab > 0, slab < slabs - 1
    groups = xcells * levels

    barrier = pltpu.get_barrier_semaphore()

    def greet(step, carry):
        pl.semaphore_signal(
            barrier, inc=1, device_id=((me + step) % peers, slab), device_id_type=MESH
        )
        return carry

    lax.fori_loop(1, peers, greet, 0)

    @pl.when(has_below)
    def _():
        pl.semaphore_signal(barrier, inc=1, device_id=(me, slab - 1), device_id_type=MESH)

    @pl.when(has_above)
    def _():
        pl.semaphore_signal(barrier, inc=1, device_id=(me, slab + 1), device_id_type=MESH)

    greeted = jnp.where(has_below, 1, 0) + jnp.where(has_above, 1, 0)
    pl.semaphore_wait(barrier, peers - 1 + greeted)

    def row_copy(step):
        target = (me + step) % peers
        return pltpu.make_async_remote_copy(
            src_ref=packed.at[target],
            dst_ref=arrived.at[step],
            send_sem=send_sem.at[step],
            recv_sem=recv_sem.at[step],
            device_id=(target, slab),
            device_id_type=MESH,
        )

    def start_rows(step, carry):
        row_copy(step).start()
        return carry

    lax.fori_loop(1, peers, start_rows, 0)

    depth = min(2048, capacity)
    bundle = 8
    lane_cells = lax.broadcasted_iota(jnp.int32, (width, depth), 0).astype(jnp.float32)

    def clear(group, carry):
        total[group] = jnp.zeros((height, width), jnp.float32)
        tail = comps // 16 * 16
        updated[group % xcells, group // xcells, tail:, :] = jnp.zeros(
            (height - tail, width), jnp.bfloat16
        )
        return carry

    lax.fori_loop(0, groups, clear, 0)

    def add_rows(source, at):
        def part(index, carry):
            columns = pl.ds(pl.multiple_of(index * depth, depth), depth)
            block = source[at, :, columns]
            tags = block[comps // 16 * 16 :, :].astype(jnp.float32)
            low = tags[comps % 16 : comps % 16 + 1]
            high = tags[comps % 16 + 1 : comps % 16 + 2]
            match = jnp.where(lane_cells == low, 1.0, 0.0).astype(jnp.bfloat16)

            def product(group, inner):
                first = group * bundle
                masks = [
                    jnp.where(high == (first + n).astype(jnp.float32), 1.0, 0.0).astype(jnp.bfloat16)
                    for n in range(bundle)
                ]
                rows = jnp.concatenate([block * mask for mask in masks], axis=0)
                sums = lax.dot_general(rows, match, NT, preferred_element_type=jnp.float32)
                total[pl.ds(first, bundle)] += sums.reshape(bundle, height, width)
                return inner

            lax.fori_loop(0, groups // bundle, product, 0)
            return carry

        lax.fori_loop(0, capacity // depth, part, 0)

    add_rows(packed, me)

    def receive(step, carry):
        row_copy(step).wait_recv()
        add_rows(arrived, step)
        return carry

    lax.fori_loop(1, peers, receive, 0)

    def finish(group, carry):
        value = base[group].astype(jnp.float32) + total[group, :comps]
        updated[group % xcells, group // xcells, :comps] = value.astype(jnp.bfloat16)
        return carry

    lax.fori_loop(0, groups, finish, 0)

    def halo_copy(which, source, target, step):
        return pltpu.make_async_remote_copy(
            src_ref=source,
            dst_ref=target,
            send_sem=halo_send.at[which],
            recv_sem=halo_recv.at[which],
            device_id=((me + step + peers) % peers, slab),
            device_id_type=MESH,
        )

    to_next = halo_copy(0, updated.at[xcells - 1], left, 1)
    to_prev = halo_copy(1, updated.at[0], right, -1)
    face_to_prev = halo_copy(2, cx.at[0], next_cx, -1)

    @pl.when(has_next)
    def _():
        to_next.start()

    @pl.when(has_prev)
    def _():
        to_prev.start()
        face_to_prev.start()

    @pl.when(jnp.logical_not(has_prev))
    def _():
        left[...] = jnp.zeros_like(left)

    @pl.when(jnp.logical_not(has_next))
    def _():
        right[...] = jnp.zeros_like(right)
        next_cx[...] = jnp.zeros_like(next_cx)

    def flow_copy(i):
        return pltpu.make_async_remote_copy(
            src_ref=flow.at[i],
            dst_ref=inflow.at[i],
            send_sem=flow_send.at[i],
            recv_sem=flow_recv.at[i],
            device_id=(me, (slab + slabs - 1) % slabs),
            device_id_type=MESH,
        )

    reach = gain[0]
    for k in range(1, levels):
        reach = reach * gain[k]

    def advect(i):
        def level(counter, current_flow):
            k = levels - 1 - counter
            row = pl.ds(k, 1)
            current = updated[i, k].astype(jnp.float32)
            before = (left[k] if i == 0 else updated[i - 1, k]).astype(jnp.float32)
            after = (right[k] if i == xcells - 1 else updated[i + 1, k]).astype(jnp.float32)
            west = cx[i, row]
            east = next_cx[row] if i == xcells - 1 else cx[i + 1, row]
            south = cy[i, row]
            flux_west = jnp.maximum(west, 0.0) * before + jnp.minimum(west, 0.0) * current
            flux_east = jnp.maximum(east, 0.0) * current + jnp.minimum(east, 0.0) * after
            below = pltpu.roll(current, 1, 1)
            flux_south = jnp.maximum(south, 0.0) * below + jnp.minimum(south, 0.0) * current
            flux_north = pltpu.roll(flux_south, width - 1, 1)
            value = current - (flux_east - flux_west) - (flux_north - flux_south)
            value = value.astype(jnp.bfloat16)
            advected[i, k] = value
            return (value.astype(jnp.float32) + current_flow) * gain[k]

        flow[i] = lax.fori_loop(0, levels, level, jnp.zeros((height, width), jnp.float32))

    def chain(i):
        @pl.when(has_above)
        def _():
            flow_copy(i).wait_recv()
            flow[i] += reach * inflow[i]

        @pl.when(jnp.logical_not(has_above))
        def _():
            inflow[i] = jnp.zeros((height, width), jnp.float32)

        @pl.when(has_below)
        def _():
            flow_copy(i).start()

    for i in range(1, xcells - 1):
        advect(i)

    @pl.when(has_prev)
    def _():
        to_next.wait_recv()

    @pl.when(has_next)
    def _():
        to_prev.wait_recv()
        face_to_prev.wait_recv()

    for i in range(1, xcells - 1):
        chain(i)
    for i in (0, xcells - 1):
        advect(i)
        chain(i)

    for i in [*range(1, xcells - 1), 0, xcells - 1]:

        def settle(counter, current):
            k = levels - 1 - counter
            value = (advected[i, k].astype(jnp.float32) + current) * scale[k]
            out[k * xcells + i] = value[:comps].astype(jnp.bfloat16)
            return (advected[i, k].astype(jnp.float32) + current) * gain[k]

        lax.fori_loop(0, levels, settle, inflow[i])

    def sent(step, carry):
        row_copy(step).wait_send()
        return carry

    lax.fori_loop(1, peers, sent, 0)

    @pl.when(has_next)
    def _():
        to_next.wait_send()

    @pl.when(has_prev)
    def _():
        to_prev.wait_send()
        face_to_prev.wait_send()

    @pl.when(has_below)
    def _():
        for i in range(xcells):
            flow_copy(i).wait_send()


def per_device(base_field, increments, dest_tile, dest_cell, courant_x, courant_y, fall_courant):
    comps, levels, xcells, ycells = base_field.shape
    row_count = increments.shape[1]
    peers = lax.axis_size("xy")
    capacity = 2 * row_count // peers
    height = up(comps + 2, 16)
    groups = levels * xcells
    block = 512

    targets = dest_tile[:, 0]
    member = (targets[None, :] == jnp.arange(peers, dtype=jnp.int32)[:, None]).astype(jnp.int32)
    counts = running_counts(member)
    slots = targets * capacity + jnp.sum(counts * member, axis=0) - 1
    starts = jnp.pad(counts[:, block - 1 :: block], ((0, 0), (1, 0)))
    low = (dest_cell % ycells).astype(jnp.bfloat16)
    high = (dest_cell // ycells).astype(jnp.bfloat16)
    rows = jnp.concatenate(
        [
            increments,
            low[None],
            high[None],
            jnp.zeros((height - comps - 2, row_count), jnp.bfloat16),
        ],
        axis=0,
    )
    vmem = pl.BlockSpec(memory_space=pltpu.VMEM)
    packed = pl.pallas_call(
        functools.partial(pack_kernel, block),
        out_shape=jax.ShapeDtypeStruct((peers, height, capacity), jnp.bfloat16),
        in_specs=[pl.BlockSpec(memory_space=pltpu.SMEM), vmem, vmem],
        out_specs=vmem,
        compiler_params=pltpu.CompilerParams(vmem_limit_bytes=48 * 2**20),
        name="pack_rows",
    )(starts, rows, slots[None])

    pad_comps = ((0, 0), (0, height - comps), (0, 0))
    base = jnp.transpose(base_field, (1, 2, 0, 3)).reshape(groups, comps, ycells)
    first = jnp.logical_and(
        lax.axis_index("xy") == 0, jnp.arange(xcells)[:, None, None] == 0
    )
    face_x = jnp.where(first, 0.0, jnp.transpose(courant_x.astype(jnp.float32), (1, 0, 2)))
    face_y = jnp.transpose(courant_y.astype(jnp.float32), (1, 0, 2))
    face_y = jnp.where(jnp.arange(ycells)[None, None, :] == 0, 0.0, face_y)
    fall = lax.dynamic_slice_in_dim(fall_courant, lax.axis_index("gz") * levels, levels, 1)
    fall = jnp.pad(jnp.transpose(fall)[:, :, None], pad_comps)
    scale = 1.0 / (1.0 + fall)
    gain = fall / (1.0 + fall)

    settled = pl.pallas_call(
        functools.partial(main_kernel, comps),
        out_shape=jax.ShapeDtypeStruct((groups, comps, ycells), jnp.bfloat16),
        in_specs=[vmem] * 6,
        out_specs=vmem,
        scratch_shapes=[
            pltpu.VMEM((peers, height, capacity), jnp.bfloat16),
            pltpu.VMEM((groups, height, ycells), jnp.float32),
            pltpu.VMEM((xcells, levels, height, ycells), jnp.bfloat16),
            pltpu.VMEM((xcells, levels, height, ycells), jnp.bfloat16),
            pltpu.VMEM((levels, height, ycells), jnp.bfloat16),
            pltpu.VMEM((levels, height, ycells), jnp.bfloat16),
            pltpu.VMEM((levels, ycells), jnp.float32),
            pltpu.VMEM((xcells, height, ycells), jnp.float32),
            pltpu.VMEM((xcells, height, ycells), jnp.float32),
            pltpu.SemaphoreType.DMA((peers,)),
            pltpu.SemaphoreType.DMA((peers,)),
            pltpu.SemaphoreType.DMA((3,)),
            pltpu.SemaphoreType.DMA((3,)),
            pltpu.SemaphoreType.DMA((xcells,)),
            pltpu.SemaphoreType.DMA((xcells,)),
        ],
        compiler_params=pltpu.CompilerParams(
            vmem_limit_bytes=56 * 2**20, collective_id=0, has_side_effects=True
        ),
        name="exchange_advect_settle",
    )(packed, base, face_x, face_y, scale, gain)
    settled = settled.reshape(levels, xcells, comps, ycells)
    return jnp.transpose(settled, (2, 0, 1, 3))


def solution(mesh):
    in_specs = (
        P(None, "gz", "xy", None),
        P(None, ("xy", "gz")),
        P(("xy", "gz"), None),
        P(("xy", "gz")),
        P("gz", "xy", None),
        P("gz", "xy", None),
        P(),
    )
    out_specs = P(None, "gz", "xy", None)
    return jax.shard_map(
        per_device, mesh=mesh, in_specs=in_specs, out_specs=out_specs, check_vma=False
    )
```

```python
import functools

import jax
import jax.numpy as jnp
from jax import lax
from jax.experimental import pallas as pl
from jax.experimental.pallas import tpu as pltpu
from jax.sharding import PartitionSpec as P

MESH = pl.DeviceIdType.MESH
NT = (((1,), (1,)), ((), ()))


def up(value, multiple):
    return -(-value // multiple) * multiple


def running_counts(member):
    tiles, count = member.shape
    run = 128
    grouped = member.astype(jnp.bfloat16).reshape(tiles * (count // run), run)
    inside = jnp.dot(
        grouped, jnp.triu(jnp.ones((run, run), jnp.bfloat16)), preferred_element_type=jnp.float32
    ).reshape(tiles, count // run, run)
    before = jnp.dot(
        inside[:, :, run - 1].astype(jnp.bfloat16),
        jnp.triu(jnp.ones((count // run, count // run), jnp.bfloat16), 1),
        preferred_element_type=jnp.float32,
    )
    return (inside + before[:, :, None]).reshape(tiles, count).astype(jnp.int32)


def pack_kernel(block, starts_ref, rows_ref, slot_ref, out_ref):
    peers, height, capacity = out_ref.shape
    width = min(256, capacity)
    blocks = rows_ref.shape[1] // block
    window = lax.broadcasted_iota(jnp.int32, (width, block), 0)

    def clear(tile, carry):
        out_ref[tile] = jnp.zeros((height, capacity), out_ref.dtype)
        return carry

    lax.fori_loop(0, peers, clear, 0)

    bundle = min(8, peers)
    windows = capacity // width

    def step(counter, carry):
        part, first_tile = counter // (peers // bundle), counter % (peers // bundle) * bundle
        columns = pl.ds(pl.multiple_of(part * block, block), block)
        slots = slot_ref[:, columns]

        def match(tile, chunk):
            base = tile * capacity + chunk * width
            return jnp.where(window == slots - base, 1.0, 0.0).astype(jnp.bfloat16)

        def move(matches):
            return lax.dot_general(
                rows_ref[:, columns], matches, NT, preferred_element_type=jnp.float32
            ).astype(out_ref.dtype)

        def spot(chunk):
            return pl.ds(pl.multiple_of(chunk * width, width), width)

        tiles = [first_tile + n for n in range(bundle)]
        chunks = [jnp.minimum(starts_ref[tile, part] // width, windows - 1) for tile in tiles]
        moved = move(jnp.concatenate([match(*pair) for pair in zip(tiles, chunks)], axis=0))
        for n in range(bundle):
            out_ref[tiles[n], :, spot(chunks[n])] += moved[:, n * width : (n + 1) * width]

        def more(tile, inner):
            start = starts_ref[tile, part]
            stop = starts_ref[tile, part + 1]

            def place(chunk, innermost):
                out_ref[tile, :, spot(chunk)] += move(match(tile, chunk))
                return innermost

            lax.fori_loop(start // width + 1, (stop + width - 1) // width, place, 0)
            return inner

        lax.fori_loop(first_tile, first_tile + bundle, more, 0)
        return carry

    lax.fori_loop(0, blocks * (peers // bundle), step, 0)


def main_kernel(
    comps, packed, base, cx, cy, scale, gain, out, arrived, total, updated, advected, left, right,
    next_cx, flow, inflow, send_sem, recv_sem, halo_send, halo_recv, flow_send, flow_recv,
):
    peers, height, capacity = packed.shape
    xcells, levels, _, width = updated.shape
    slabs = lax.axis_size("gz")
    me, slab = lax.axis_index("xy"), lax.axis_index("gz")
    has_prev, has_next = me > 0, me < peers - 1
    has_below, has_above = slab > 0, slab < slabs - 1
    groups = xcells * levels

    barrier = pltpu.get_barrier_semaphore()

    def greet(step, carry):
        pl.semaphore_signal(
            barrier, inc=1, device_id=((me + step) % peers, slab), device_id_type=MESH
        )
        return carry

    lax.fori_loop(1, peers, greet, 0)

    @pl.when(has_below)
    def _():
        pl.semaphore_signal(barrier, inc=1, device_id=(me, slab - 1), device_id_type=MESH)

    @pl.when(has_above)
    def _():
        pl.semaphore_signal(barrier, inc=1, device_id=(me, slab + 1), device_id_type=MESH)

    greeted = jnp.where(has_below, 1, 0) + jnp.where(has_above, 1, 0)
    pl.semaphore_wait(barrier, peers - 1 + greeted)

    def row_copy(step):
        target = (me + step) % peers
        return pltpu.make_async_remote_copy(
            src_ref=packed.at[target],
            dst_ref=arrived.at[step],
            send_sem=send_sem.at[step],
            recv_sem=recv_sem.at[step],
            device_id=(target, slab),
            device_id_type=MESH,
        )

    def start_rows(step, carry):
        row_copy(step).start()
        return carry

    lax.fori_loop(1, peers, start_rows, 0)

    depth = min(2048, capacity)
    bundle = 8
    lane_cells = lax.broadcasted_iota(jnp.int32, (width, depth), 0).astype(jnp.float32)

    def clear(group, carry):
        total[group] = jnp.zeros((height, width), jnp.float32)
        tail = comps // 16 * 16
        updated[group % xcells, group // xcells, tail:, :] = jnp.zeros(
            (height - tail, width), jnp.bfloat16
        )
        return carry

    lax.fori_loop(0, groups, clear, 0)

    def add_rows(source, at):
        def part(index, carry):
            columns = pl.ds(pl.multiple_of(index * depth, depth), depth)
            block = source[at, :, columns]
            tags = block[comps // 16 * 16 :, :].astype(jnp.float32)
            low = tags[comps % 16 : comps % 16 + 1]
            high = tags[comps % 16 + 1 : comps % 16 + 2]
            match = jnp.where(lane_cells == low, 1.0, 0.0).astype(jnp.bfloat16)

            def product(group, inner):
                first = group * bundle
                masks = [
                    jnp.where(high == (first + n).astype(jnp.float32), 1.0, 0.0).astype(jnp.bfloat16)
                    for n in range(bundle)
                ]
                rows = jnp.concatenate([block * mask for mask in masks], axis=0)
                sums = lax.dot_general(rows, match, NT, preferred_element_type=jnp.float32)
                total[pl.ds(first, bundle)] += sums.reshape(bundle, height, width)
                return inner

            lax.fori_loop(0, groups // bundle, product, 0)
            return carry

        lax.fori_loop(0, capacity // depth, part, 0)

    add_rows(packed, me)

    def receive(step, carry):
        row_copy(step).wait_recv()
        add_rows(arrived, step)
        return carry

    lax.fori_loop(1, peers, receive, 0)

    def finish(group, carry):
        value = base[group].astype(jnp.float32) + total[group, :comps]
        updated[group % xcells, group // xcells, :comps] = value.astype(jnp.bfloat16)
        return carry

    lax.fori_loop(0, groups, finish, 0)

    def halo_copy(which, source, target, step):
        return pltpu.make_async_remote_copy(
            src_ref=source,
            dst_ref=target,
            send_sem=halo_send.at[which],
            recv_sem=halo_recv.at[which],
            device_id=((me + step + peers) % peers, slab),
            device_id_type=MESH,
        )

    to_next = halo_copy(0, updated.at[xcells - 1], left, 1)
    to_prev = halo_copy(1, updated.at[0], right, -1)
    face_to_prev = halo_copy(2, cx.at[0], next_cx, -1)

    @pl.when(has_next)
    def _():
        to_next.start()

    @pl.when(has_prev)
    def _():
        to_prev.start()
        face_to_prev.start()

    @pl.when(jnp.logical_not(has_prev))
    def _():
        left[...] = jnp.zeros_like(left)

    @pl.when(jnp.logical_not(has_next))
    def _():
        right[...] = jnp.zeros_like(right)
        next_cx[...] = jnp.zeros_like(next_cx)

    def flow_copy(i):
        return pltpu.make_async_remote_copy(
            src_ref=flow.at[i],
            dst_ref=inflow.at[i],
            send_sem=flow_send.at[i],
            recv_sem=flow_recv.at[i],
            device_id=(me, (slab + slabs - 1) % slabs),
            device_id_type=MESH,
        )

    reach = gain[0]
    for k in range(1, levels):
        reach = reach * gain[k]

    def advect(i):
        def level(counter, current_flow):
            k = levels - 1 - counter
            row = pl.ds(k, 1)
            current = updated[i, k].astype(jnp.float32)
            before = (left[k] if i == 0 else updated[i - 1, k]).astype(jnp.float32)
            after = (right[k] if i == xcells - 1 else updated[i + 1, k]).astype(jnp.float32)
            west = cx[i, row]
            east = next_cx[row] if i == xcells - 1 else cx[i + 1, row]
            south = cy[i, row]
            flux_west = jnp.maximum(west, 0.0) * before + jnp.minimum(west, 0.0) * current
            flux_east = jnp.maximum(east, 0.0) * current + jnp.minimum(east, 0.0) * after
            below = pltpu.roll(current, 1, 1)
            flux_south = jnp.maximum(south, 0.0) * below + jnp.minimum(south, 0.0) * current
            flux_north = pltpu.roll(flux_south, width - 1, 1)
            value = current - (flux_east - flux_west) - (flux_north - flux_south)
            value = value.astype(jnp.bfloat16)
            advected[i, k] = value
            return (value.astype(jnp.float32) + current_flow) * gain[k]

        flow[i] = lax.fori_loop(0, levels, level, jnp.zeros((height, width), jnp.float32))

    def chain(i):
        @pl.when(has_above)
        def _():
            flow_copy(i).wait_recv()
            flow[i] += reach * inflow[i]

        @pl.when(jnp.logical_not(has_above))
        def _():
            inflow[i] = jnp.zeros((height, width), jnp.float32)

        @pl.when(has_below)
        def _():
            flow_copy(i).start()

    for i in range(1, xcells - 1):
        advect(i)

    @pl.when(has_prev)
    def _():
        to_next.wait_recv()

    @pl.when(has_next)
    def _():
        to_prev.wait_recv()
        face_to_prev.wait_recv()

    for i in range(1, xcells - 1):
        chain(i)
    for i in (0, xcells - 1):
        advect(i)
        chain(i)

    for i in [*range(1, xcells - 1), 0, xcells - 1]:

        def settle(counter, current):
            k = levels - 1 - counter
            value = (advected[i, k].astype(jnp.float32) + current) * scale[k]
            out[k * xcells + i] = value[:comps].astype(jnp.bfloat16)
            return (advected[i, k].astype(jnp.float32) + current) * gain[k]

        lax.fori_loop(0, levels, settle, inflow[i])

    def sent(step, carry):
        row_copy(step).wait_send()
        return carry

    lax.fori_loop(1, peers, sent, 0)

    @pl.when(has_next)
    def _():
        to_next.wait_send()

    @pl.when(has_prev)
    def _():
        to_prev.wait_send()
        face_to_prev.wait_send()

    @pl.when(has_below)
    def _():
        for i in range(xcells):
            flow_copy(i).wait_send()


def per_device(base_field, increments, dest_tile, dest_cell, courant_x, courant_y, fall_courant):
    comps, levels, xcells, ycells = base_field.shape
    row_count = increments.shape[1]
    peers = lax.axis_size("xy")
    capacity = 2 * row_count // peers
    height = up(comps + 2, 16)
    groups = levels * xcells
    block = 256

    targets = dest_tile[:, 0]
    member = (targets[None, :] == jnp.arange(peers, dtype=jnp.int32)[:, None]).astype(jnp.int32)
    counts = running_counts(member)
    slots = targets * capacity + jnp.sum(counts * member, axis=0) - 1
    starts = jnp.pad(counts[:, block - 1 :: block], ((0, 0), (1, 0)))
    low = (dest_cell % ycells).astype(jnp.bfloat16)
    high = (dest_cell // ycells).astype(jnp.bfloat16)
    rows = jnp.concatenate(
        [
            increments,
            low[None],
            high[None],
            jnp.zeros((height - comps - 2, row_count), jnp.bfloat16),
        ],
        axis=0,
    )
    vmem = pl.BlockSpec(memory_space=pltpu.VMEM)
    packed = pl.pallas_call(
        functools.partial(pack_kernel, block),
        out_shape=jax.ShapeDtypeStruct((peers, height, capacity), jnp.bfloat16),
        in_specs=[pl.BlockSpec(memory_space=pltpu.SMEM), vmem, vmem],
        out_specs=vmem,
        compiler_params=pltpu.CompilerParams(vmem_limit_bytes=48 * 2**20),
        name="pack_rows",
    )(starts, rows, slots[None])

    pad_comps = ((0, 0), (0, height - comps), (0, 0))
    base = jnp.transpose(base_field, (1, 2, 0, 3)).reshape(groups, comps, ycells)
    first = jnp.logical_and(
        lax.axis_index("xy") == 0, jnp.arange(xcells)[:, None, None] == 0
    )
    face_x = jnp.where(first, 0.0, jnp.transpose(courant_x.astype(jnp.float32), (1, 0, 2)))
    face_y = jnp.transpose(courant_y.astype(jnp.float32), (1, 0, 2))
    face_y = jnp.where(jnp.arange(ycells)[None, None, :] == 0, 0.0, face_y)
    fall = lax.dynamic_slice_in_dim(fall_courant, lax.axis_index("gz") * levels, levels, 1)
    fall = jnp.pad(jnp.transpose(fall)[:, :, None], pad_comps)
    scale = 1.0 / (1.0 + fall)
    gain = fall / (1.0 + fall)

    settled = pl.pallas_call(
        functools.partial(main_kernel, comps),
        out_shape=jax.ShapeDtypeStruct((groups, comps, ycells), jnp.bfloat16),
        in_specs=[vmem] * 6,
        out_specs=vmem,
        scratch_shapes=[
            pltpu.VMEM((peers, height, capacity), jnp.bfloat16),
            pltpu.VMEM((groups, height, ycells), jnp.float32),
            pltpu.VMEM((xcells, levels, height, ycells), jnp.bfloat16),
            pltpu.VMEM((xcells, levels, height, ycells), jnp.bfloat16),
            pltpu.VMEM((levels, height, ycells), jnp.bfloat16),
            pltpu.VMEM((levels, height, ycells), jnp.bfloat16),
            pltpu.VMEM((levels, ycells), jnp.float32),
            pltpu.VMEM((xcells, height, ycells), jnp.float32),
            pltpu.VMEM((xcells, height, ycells), jnp.float32),
            pltpu.SemaphoreType.DMA((peers,)),
            pltpu.SemaphoreType.DMA((peers,)),
            pltpu.SemaphoreType.DMA((3,)),
            pltpu.SemaphoreType.DMA((3,)),
            pltpu.SemaphoreType.DMA((xcells,)),
            pltpu.SemaphoreType.DMA((xcells,)),
        ],
        compiler_params=pltpu.CompilerParams(
            vmem_limit_bytes=56 * 2**20, collective_id=0, has_side_effects=True
        ),
        name="exchange_advect_settle",
    )(packed, base, face_x, face_y, scale, gain)
    settled = settled.reshape(levels, xcells, comps, ycells)
    return jnp.transpose(settled, (2, 0, 1, 3))


def solution(mesh):
    in_specs = (
        P(None, "gz", "xy", None),
        P(None, ("xy", "gz")),
        P(("xy", "gz"), None),
        P(("xy", "gz")),
        P("gz", "xy", None),
        P("gz", "xy", None),
        P(),
    )
    out_specs = P(None, "gz", "xy", None)
    return jax.shard_map(
        per_device, mesh=mesh, in_specs=in_specs, out_specs=out_specs, check_vma=False
    )
```
